32 devices in a mesh: dp: 4 (over z), fsdp: 4 (over x, core), seq: 2 (over y).
Axes of the slice: x: 2, y: 2, z: 4, core: 2. Of those that a mesh axis runs over, the one named last changes fastest.
Arguments:
- hidden_in: bfloat16 [16, 1024, 1024], P(('dp', 'fsdp'), 'seq'), may hold values from -6 to 6
- lengths: int32 [16, 4], P(('dp', 'fsdp')), may hold values from 0 to 1024, as said below
- ln1_gain: bfloat16 [1024], P('fsdp'), may hold values from 0.25 to 1.75
- ln1_bias: bfloat16 [1024], P('fsdp'), may hold values from -1.5 to 1.5
- qkv_weight: bfloat16 [1024, 3072], P('fsdp'), may hold values from -0.1875 to 0.1875
- qv_bias: bfloat16 [2048], P('fsdp'), may hold values from -2.5 to 2.5
- dense_weight: bfloat16 [1024, 1024], P('fsdp'), may hold values from -0.25 to 0.25
- dense_bias: bfloat16 [1024], P('fsdp'), may hold values from -1.5 to 1.5
- ln2_gain: bfloat16 [1024], P('fsdp'), may hold values from 0.25 to 1.75
- ln2_bias: bfloat16 [1024], P('fsdp'), may hold values from -1.5 to 1.5
- fc1_weight: bfloat16 [1024, 4096], P('fsdp'), may hold values from -0.1875 to 0.1875
- fc1_bias: bfloat16 [4096], P('fsdp'), may hold values from -2.5 to 2.5
- fc2_weight: bfloat16 [4096, 1024], P('fsdp'), may hold values from -0.125 to 0.125
- fc2_bias: bfloat16 [1024], P('fsdp'), may hold values from -1.5 to 1.5
- cotangent: bfloat16 [16, 1024, 1024], P(('dp', 'fsdp'), 'seq'), may hold values from -12 to 12
Outputs:
- output: bfloat16 [16, 1024, 1024], P(('dp', 'fsdp'), 'seq')
- grad_input: bfloat16 [16, 1024, 1024], P(('dp', 'fsdp'), 'seq')
- grad_ln1_gain: float32 [1024], P('fsdp')
- grad_ln1_bias: float32 [1024], P('fsdp')
- grad_qkv_weight: float32 [1024, 3072], P('fsdp')
- grad_qv_bias: float32 [2048], P('fsdp')
- grad_dense_weight: float32 [1024, 1024], P('fsdp')
- grad_dense_bias: float32 [1024], P('fsdp')
- grad_ln2_gain: float32 [1024], P('fsdp')
- grad_ln2_bias: float32 [1024], P('fsdp')
- grad_fc1_weight: float32 [1024, 4096], P('fsdp')
- grad_fc1_bias: float32 [4096], P('fsdp')
- grad_fc2_weight: float32 [4096, 1024], P('fsdp')
- grad_fc2_bias: float32 [1024], P('fsdp')
The draws below stay inside these ranges and needn't reach their ends.
Inputs may be any that keep to these rules, and one draw needn't show every extreme that they name: Row r lists, in order, the lengths of the 4 documents packed into slot r; they sum to 1024, and a length may be 0. Of the 1 row of each group of devices along seq, one, drawn from the seed, begins with a document longer than 1024 - 1024 // 2 tokens; one row of the whole array, drawn from the seed, holds a single document of 1024 tokens.
All inputs are finite; a program needn't handle non-finite values.
Results may differ from the reference program's by a relative error of at most 0.015.
Values may be sent and summed in bfloat16 or wider, within the bound.
A program may use at most 192 MiB of HBM per device.

```python
import math
from functools import partial
import jax
import jax.numpy as jnp
from jax import lax

H = 16
HD = 64
FF = 4096
DOCS = 4
D = 1024
LENGTH = 1024
SEQS = 1
NSEQ = 16
Q_BLOCK = 512
N_SEQ = 2


def draw_lengths(key, part):
    key = jax.random.fold_in(key, 5)
    cut_key, pick_key, long_key, full_key = jax.random.split(key, 4)
    cut_points = jnp.sort(jax.random.randint(cut_key, (NSEQ, DOCS - 1), 1, LENGTH), axis=1).astype(jnp.int32)
    bounds = jnp.concatenate([jnp.zeros((NSEQ, 1), jnp.int32), cut_points, jnp.full((NSEQ, 1), LENGTH, jnp.int32)], axis=1)
    pieces = bounds[:, 1:] - bounds[:, :-1]
    chosen = jax.random.randint(pick_key, (NSEQ // SEQS,), 0, SEQS).astype(jnp.int32)
    slot_index = jnp.arange(NSEQ, dtype=jnp.int32)
    whole_row = slot_index % SEQS == jnp.repeat(chosen, SEQS)
    first_len = jax.random.randint(long_key, (NSEQ, 1), LENGTH - LENGTH // N_SEQ + 1, LENGTH).astype(jnp.int32)
    spanning = jnp.concatenate([first_len, LENGTH - first_len, jnp.zeros((NSEQ, DOCS - 2), jnp.int32)], axis=1)
    single = jnp.concatenate([jnp.full((NSEQ, 1), LENGTH, jnp.int32), jnp.zeros((NSEQ, DOCS - 1), jnp.int32)], axis=1)
    full_pick = jax.random.randint(full_key, (), 0, NSEQ).astype(jnp.int32)
    mixed_rows = jnp.where(whole_row[:, None], spanning, pieces)
    return jnp.where((slot_index == full_pick)[:, None], single, mixed_rows).astype(jnp.int32)


def draw_cotangent(key, part):
    key = jax.random.fold_in(key, 9)
    base_key = jax.random.fold_in(key, 0)
    seq_frac = jnp.arange(NSEQ, dtype=jnp.float32) / NSEQ
    pos_frac = jnp.arange(LENGTH, dtype=jnp.float32) / LENGTH
    rise_factor = jnp.exp(jnp.log(3.0) * (seq_frac[:, None] + pos_frac[None, :])) / 3.0
    noise_part = jnp.clip(jax.random.normal(base_key, (NSEQ, LENGTH, D), jnp.float32), -4.0, 4.0)
    values = noise_part * rise_factor[:, :, None]
    return values.astype(jnp.bfloat16)


def steps_of(key, extent, cuts, smallest, high):
    def one(axis_at, shards_of):
        draws = jax.random.uniform(jax.random.fold_in(jax.random.fold_in(key, 6), axis_at), (shards_of,), jnp.float32, smallest / len(cuts), high / len(cuts))
        return jnp.repeat(jnp.exp(draws), extent[axis_at] // shards_of).reshape((-1,) + (1,) * (len(extent) - axis_at - 1))

    level = one(*cuts[0])
    for cut in cuts[1:]:
        level = level * one(*cut)
    return level


def gaussian(rng, dims, width, most, cuts=(), kind=jnp.bfloat16):
    gain = steps_of(rng, dims, cuts, -0.22, 0.18) if cuts else 1.0
    entries = jax.random.normal(rng, dims, jnp.float32) * width * gain
    return jnp.minimum(jnp.maximum(entries, -most), most).astype(kind)


def setup_inputs(seed: int = 0) -> dict:
    key_of = jax.random.split(jax.random.key(seed), 16)
    hidden_in = gaussian(key_of[0], (NSEQ, LENGTH, D), 1.0, 6.0, ((0, 16), (1, 2)))
    lengths = draw_lengths(jax.random.fold_in(key_of[15], 71), 0)
    ln1_gain = jnp.clip(1.0 + 0.15 * jax.random.normal(key_of[2], (D,), jnp.float32), 0.25, 1.75).astype(jnp.bfloat16)
    ln1_bias = gaussian(key_of[3], (D,), 0.3, 1.5, ((0, 4),))
    qkv_weight = gaussian(key_of[4], (D, 3 * D), D ** -0.5, 0.1875, ((0, 4),))
    qv_bias = gaussian(key_of[5], (2 * D,), 0.5, 2.5, ((0, 4),))
    dense_weight = gaussian(key_of[6], (D, D), (D // 2) ** -0.5, 0.25, ((0, 4),))
    dense_bias = gaussian(key_of[7], (D,), 0.3, 1.5, ((0, 4),))
    ln2_gain = jnp.clip(1.0 + 0.15 * jax.random.normal(key_of[8], (D,), jnp.float32), 0.25, 1.75).astype(jnp.bfloat16)
    ln2_bias = gaussian(key_of[9], (D,), 0.3, 1.5, ((0, 4),))
    fc1_weight = gaussian(key_of[10], (D, FF), D ** -0.5, 0.1875, ((0, 4),))
    fc1_bias = gaussian(key_of[11], (FF,), 0.5, 2.5, ((0, 4),))
    fc2_weight = gaussian(key_of[12], (FF, D), (FF // 2) ** -0.5, 0.125, ((0, 4),))
    fc2_bias = gaussian(key_of[13], (D,), 0.3, 1.5, ((0, 4),))
    cotangent = draw_cotangent(jax.random.fold_in(key_of[15], 71), 0)
    return dict(hidden_in=hidden_in, lengths=lengths, ln1_gain=ln1_gain, ln1_bias=ln1_bias, qkv_weight=qkv_weight, qv_bias=qv_bias, dense_weight=dense_weight, dense_bias=dense_bias, ln2_gain=ln2_gain, ln2_bias=ln2_bias, fc1_weight=fc1_weight, fc1_bias=fc1_bias, fc2_weight=fc2_weight, fc2_bias=fc2_bias, cotangent=cotangent)


@jax.custom_vjp
def low(v):
    return lax.optimization_barrier(v.astype(jnp.bfloat16)).astype(jnp.float32)

@jax.custom_vjp
def low_back(v):
    return v

def low_keep(v):
    return (low(v), None)

def low_pass(kept, grad):
    return (grad,)

def back_keep(v):
    return (v, None)

def back_low(kept, grad):
    return (low(grad),)
low.defvjp(low_keep, low_pass)
low_back.defvjp(back_keep, back_low)
EPSILON = 1e-05
PRECISE = lax.Precision.HIGHEST
GELU_COEF = 0.7978845608028654

def norm_layer(values, gain_vec, shift_vec):
    row_mean = lax.optimization_barrier(jnp.mean(values, axis=-1, keepdims=True))
    centered = values - row_mean
    variance = lax.optimization_barrier(jnp.mean(centered * centered, axis=-1, keepdims=True))
    return centered * lax.rsqrt(variance + EPSILON) * gain_vec + shift_vec

def gelu_tanh(values):
    return 0.5 * values * (1.0 + jnp.tanh(GELU_COEF * (values + 0.044715 * values * values * values)))

def doc_numbers(length_row):
    doc_ends = jnp.cumsum(length_row).astype(jnp.int32)
    positions = jnp.arange(LENGTH, dtype=jnp.int32)
    return lax.optimization_barrier(jnp.sum((positions[:, None] >= doc_ends[None, :]).astype(jnp.int32), axis=1)).astype(jnp.int32)

def expand_bias(pair_bias):
    grouped = pair_bias.reshape(H, 2, HD)
    zero_keys = jnp.zeros((H, 1, HD), grouped.dtype)
    return jnp.concatenate([grouped[:, :1], zero_keys, grouped[:, 1:]], axis=1).reshape(3 * H * HD)

def head_slopes():
    return 2.0 ** (-8.0 * jnp.arange(1, H + 1).astype(jnp.float32) / H)

def attend_block(row_start, query_rows, key_rows, value_rows, doc_of, slopes):
    query_pos = row_start + jnp.arange(Q_BLOCK, dtype=jnp.int32)
    key_pos = jnp.arange(LENGTH, dtype=jnp.int32)
    block_query = lax.dynamic_slice_in_dim(query_rows, row_start, Q_BLOCK, 0)
    query_doc = lax.dynamic_slice_in_dim(doc_of, row_start, Q_BLOCK, 0)
    raw_scores = jnp.einsum('qhd,khd->hqk', block_query, key_rows, precision=PRECISE) * (1.0 / math.sqrt(HD))
    offsets = (key_pos[None, :] - query_pos[:, None]).astype(jnp.float32)
    raw_scores = low_back(raw_scores + slopes[:, None, None] * offsets[None])
    allowed = (key_pos[None, :] <= query_pos[:, None]) & (doc_of[None, :] == query_doc[:, None])
    masked = jnp.where(allowed[None], raw_scores, -1e+30)
    row_max = lax.optimization_barrier(jnp.max(masked, axis=-1, keepdims=True))
    exp_terms = jnp.exp(masked - row_max)
    attn_probs = low(exp_terms / lax.optimization_barrier(jnp.sum(exp_terms, axis=-1, keepdims=True)))
    return jnp.einsum('hqk,khd->qhd', attn_probs, value_rows, precision=PRECISE)

def attention(mixed_cols, length_row):
    split_cols = mixed_cols.reshape(LENGTH, H, 3, HD)
    query_rows = split_cols[:, :, 0]
    key_rows = split_cols[:, :, 1]
    value_rows = split_cols[:, :, 2]
    doc_of = doc_numbers(length_row)
    slopes = head_slopes()

    def one_block(row_start):
        return attend_block(row_start, query_rows, key_rows, value_rows, doc_of, slopes)
    starts = jnp.arange(LENGTH // Q_BLOCK, dtype=jnp.int32) * Q_BLOCK
    outputs = lax.map(jax.checkpoint(one_block), starts)
    return outputs.reshape(LENGTH, H * HD)

def layer(params, tokens, length_row):
    gain_one, shift_one, w_mixed, pair_bias, w_dense, bias_dense, gain_two, shift_two, w_up, bias_up, w_down, bias_down = params
    normed = low(norm_layer(tokens, gain_one, shift_one))
    mixed_cols = low(low_back(jnp.dot(normed, w_mixed, precision=PRECISE) + expand_bias(pair_bias)))
    attended = low(low_back(attention(mixed_cols, length_row)))
    hidden = tokens + low_back(jnp.dot(attended, w_dense, precision=PRECISE)) + bias_dense
    normed_two = low(norm_layer(hidden, gain_two, shift_two))
    activation = low_back(jnp.dot(normed_two, w_up, precision=PRECISE)) + bias_up
    gelu_out = low(gelu_tanh(activation))
    return hidden + jnp.dot(gelu_out, w_down, precision=PRECISE) + bias_down

def reference(hidden_in, lengths, ln1_gain, ln1_bias, qkv_weight, qv_bias, dense_weight, dense_bias, ln2_gain, ln2_bias, fc1_weight, fc1_bias, fc2_weight, fc2_bias, cotangent):
    params = tuple((member.astype(jnp.float32) for member in (ln1_gain, ln1_bias, qkv_weight, qv_bias, dense_weight, dense_bias, ln2_gain, ln2_bias, fc1_weight, fc1_bias, fc2_weight, fc2_bias)))
    tokens = hidden_in.astype(jnp.float32)

    def forward(param_set, token_set):
        step_fn = jax.checkpoint(partial(layer, param_set))

        def one_sequence(paired):
            return step_fn(paired[0], paired[1])
        return lax.map(one_sequence, (token_set, lengths))
    result, pullback = jax.vjp(forward, params, tokens)
    param_grads, token_grad = pullback(cotangent.astype(jnp.float32))
    g_gain_one, g_shift_one, g_w_mixed, g_pair_bias, g_w_dense, g_bias_dense, g_gain_two, g_shift_two, g_w_up, g_bias_up, g_w_down, g_bias_down = param_grads
    return (result.astype(jnp.bfloat16), token_grad.astype(jnp.bfloat16), g_gain_one, g_shift_one, g_w_mixed, g_pair_bias, g_w_dense, g_bias_dense, g_gain_two, g_shift_two, g_w_up, g_bias_up, g_w_down, g_bias_down)
```

```python
import functools
import math

import jax
import jax.numpy as jnp
from jax import lax
from jax.experimental import pallas as pl
from jax.experimental.pallas import tpu as pltpu
from jax.sharding import PartitionSpec as P

H = 16
HD = 64
ROWS = 256
VMEM = 48 * 1024 * 1024


EPSILON = 1e-05
GELU_COEF = 0.7978845608028654


def norm_layer(values, gain_vec, shift_vec):
    row_mean = jnp.mean(values, axis=-1, keepdims=True)
    centered = values - row_mean
    variance = jnp.mean(centered * centered, axis=-1, keepdims=True)
    return centered * lax.rsqrt(variance + EPSILON) * gain_vec + shift_vec


def gelu_tanh(values):
    return (
        0.5 * values * (1.0 + jnp.tanh(GELU_COEF * (values + 0.044715 * values * values * values)))
    )


def contract_rows(left_side, right_side):
    return lax.dot_general(
        left_side, right_side, (((0,), (0,)), ((), ())), preferred_element_type=jnp.float32
    )


def contract_cols(left_side, right_side):
    return lax.dot_general(
        left_side, right_side, (((1,), (1,)), ((), ())), preferred_element_type=jnp.float32
    )


def steps_of(axis):
    size = lax.axis_size(axis)
    return [2**k for k in range(size.bit_length() - 1)]


def bit_of(axis, step):
    return lax.rem(lax.axis_index(axis) // step, 2)


def swap(value, axis, step):
    pairs = [(i, i ^ step) for i in range(lax.axis_size(axis))]
    return lax.ppermute(value, axis, pairs)


def pick(value, dim, index):
    return lax.dynamic_index_in_dim(value, index, dim, keepdims=False)


def halve(value, axis, step, dim):
    bit = bit_of(axis, step)
    received = swap(pick(value, dim, 1 - bit), axis, step)
    kept = pick(value, dim, bit).astype(jnp.float32)
    return (kept + received.astype(jnp.float32)).astype(jnp.bfloat16)


def double(value, axis, step, dim):
    other = swap(value, axis, step)
    first = jnp.stack([value, other], axis=dim)
    second = jnp.stack([other, value], axis=dim)
    return jnp.where(bit_of(axis, step) == 0, first, second)


def gather(value, axis):
    shape = value.shape
    value = value[None]
    for step in steps_of(axis):
        value = double(value, axis, step, 0).reshape((-1,) + shape)
    return value


def reduce_rows(grad, order, axes):
    labels = [(axis, step) for axis in axes for step in reversed(steps_of(axis))]
    columns = grad.shape[1]
    value = grad.reshape((2,) * len(labels) + (-1, columns))
    for label in order:
        value = halve(value, label[0], label[1], labels.index(label))
        labels.remove(label)
    return value


def labels_of(*axes):
    return [(axis, step) for axis in axes for step in steps_of(axis)]


def spread_rows(value, axes):
    columns = value.shape[-1]
    for axis in reversed(axes):
        for place, step in enumerate(reversed(steps_of(axis))):
            value = double(value, axis, step, place)
        value = value.reshape(-1, columns)
    return value


def sum_all(value, axes):
    for axis in axes:
        for step in steps_of(axis):
            value = value + swap(value, axis, step)
    return value


def doc_starts_of(lengths, seq_length):
    ends = jnp.cumsum(lengths, axis=1)
    positions = jnp.arange(seq_length, dtype=jnp.int32)
    passed = ends[:, :, None] <= positions[None, None, :]
    return jnp.max(jnp.where(passed, ends[:, :, None], 0), axis=1, keepdims=True)


def local_columns(pair_bias, heads_here):
    first = lax.axis_index("seq") * heads_here
    grouped = lax.dynamic_slice_in_dim(pair_bias.reshape(H, 2, HD), first, heads_here, 0)
    zeros = jnp.zeros((heads_here, 1, HD), grouped.dtype)
    stacked = jnp.concatenate([grouped[:, :1], zeros, grouped[:, 1:]], axis=1)
    return stacked.reshape(heads_here * 3 * HD)


def pack(parts):
    return jnp.concatenate(parts).reshape(-1, 128)


def attend_forward_kernel(starts_ref, slopes_ref, mixed_ref, out_ref, sums_ref, *, block, heads):
    length = mixed_ref.shape[1]
    pair = pl.program_id(1)
    for head in range(heads):
        slope = slopes_ref[pair * heads + head]
        base = head * 3 * HD
        keys = mixed_ref[0, :, base + HD : base + 2 * HD]
        values_t = mixed_ref[0, :, base + 2 * HD : base + 3 * HD].T
        for start in range(0, length, block):
            stop = start + block
            query = mixed_ref[0, start:stop, base : base + HD] * jnp.bfloat16(1 / math.sqrt(HD))
            offsets = masked_offsets(starts_ref[0, :, start:stop], start, stop, block)
            scores = contract_cols(keys[:stop], query) + slope * offsets
            row_max = jnp.max(scores, axis=0, keepdims=True)
            terms = jnp.exp(scores - row_max)
            total = jnp.sum(terms, axis=0, keepdims=True)
            probs = (terms * (1.0 / total)).astype(jnp.bfloat16)
            attended = jnp.dot(
                values_t[:, :stop], probs, preferred_element_type=jnp.float32
            )
            out_ref[0, start:stop, head * HD : (head + 1) * HD] = attended.T.astype(jnp.bfloat16)
            sums_ref[0, 0, head : head + 1, start:stop] = row_max + jnp.log(total)


def masked_offsets(doc_starts, start, stop, block):
    key_pos = lax.broadcasted_iota(jnp.int32, (stop, block), 0)
    query_pos = lax.broadcasted_iota(jnp.int32, (stop, block), 1) + start
    allowed = (key_pos <= query_pos) & (key_pos >= doc_starts)
    return jnp.where(allowed, (key_pos - query_pos).astype(jnp.float32), -1e32)


def attend_backward_kernel(
    starts_ref, slopes_ref, mixed_ref, grad_ref, sums_ref, out_ref, keys_acc, values_acc, *, block, heads
):
    length = mixed_ref.shape[1]
    pair = pl.program_id(1)
    scale = 1 / math.sqrt(HD)
    for head in range(heads):
        slope = slopes_ref[pair * heads + head]
        base = head * 3 * HD
        keys = mixed_ref[0, :, base + HD : base + 2 * HD]
        keys_t = keys.T
        values = mixed_ref[0, :, base + 2 * HD : base + 3 * HD]
        for start in reversed(range(0, length, block)):
            stop = start + block
            query = mixed_ref[0, start:stop, base : base + HD] * jnp.bfloat16(scale)
            grad = grad_ref[0, start:stop, head * HD : (head + 1) * HD]
            offsets = masked_offsets(starts_ref[0, :, start:stop], start, stop, block)
            scores = contract_cols(keys[:stop], query) + slope * offsets
            probs = jnp.exp(scores - sums_ref[0, 0, head : head + 1, start:stop])
            grad_probs = contract_cols(values[:stop], grad)
            inner = jnp.sum(grad_probs * probs, axis=0, keepdims=True)
            grad_scores = (probs * (grad_probs - inner)).astype(jnp.bfloat16)
            grad_query = jnp.dot(
                keys_t[:, :stop], grad_scores, preferred_element_type=jnp.float32
            )
            out_ref[0, start:stop, base : base + HD] = (grad_query.T * scale).astype(jnp.bfloat16)
            grad_keys = jnp.dot(grad_scores, query, preferred_element_type=jnp.float32)
            grad_values = jnp.dot(
                probs.astype(jnp.bfloat16), grad, preferred_element_type=jnp.float32
            )
            if stop == length:
                keys_acc[...] = grad_keys
                values_acc[...] = grad_values
            else:
                keys_acc[:stop] += grad_keys
                values_acc[:stop] += grad_values
        out_ref[0, :, base + HD : base + 2 * HD] = keys_acc[...].astype(jnp.bfloat16)
        out_ref[0, :, base + 2 * HD : base + 3 * HD] = values_acc[...].astype(jnp.bfloat16)


def attention_specs(length, heads):
    return [
        pl.BlockSpec((1, 1, length), lambda s, p: (s, 0, 0)),
        pl.BlockSpec(memory_space=pltpu.SMEM),
        pl.BlockSpec((1, length, heads * 3 * HD), lambda s, p: (s, 0, p)),
    ]


def attend_forward(mixed, doc_starts, slopes):
    seqs, length, columns = mixed.shape
    heads_here = columns // (3 * HD)
    heads = min(2, heads_here)
    pairs = heads_here // heads
    return pl.pallas_call(
        functools.partial(attend_forward_kernel, block=min(ROWS, length), heads=heads),
        grid=(seqs, pairs),
        in_specs=attention_specs(length, heads),
        out_specs=[
            pl.BlockSpec((1, length, heads * HD), lambda s, p: (s, 0, p)),
            pl.BlockSpec((1, 1, heads, length), lambda s, p: (s, p, 0, 0)),
        ],
        out_shape=[
            jax.ShapeDtypeStruct((seqs, length, heads_here * HD), jnp.bfloat16),
            jax.ShapeDtypeStruct((seqs, pairs, heads, length), jnp.float32),
        ],
        compiler_params=pltpu.CompilerParams(vmem_limit_bytes=VMEM),
        cost_estimate=pl.CostEstimate(
            flops=seqs * heads_here * length * length * HD * 8,
            bytes_accessed=seqs * length * columns * 4,
            transcendentals=seqs * heads_here * length * length,
        ),
    )(doc_starts, slopes, mixed)


def attend_backward(mixed, grad, sums, doc_starts, slopes):
    seqs, length, columns = mixed.shape
    heads_here = columns // (3 * HD)
    heads = min(2, heads_here)
    pairs = heads_here // heads
    return pl.pallas_call(
        functools.partial(attend_backward_kernel, block=min(ROWS, length), heads=heads),
        grid=(seqs, pairs),
        in_specs=attention_specs(length, heads)
        + [
            pl.BlockSpec((1, length, heads * HD), lambda s, p: (s, 0, p)),
            pl.BlockSpec((1, 1, heads, length), lambda s, p: (s, p, 0, 0)),
        ],
        out_specs=pl.BlockSpec((1, length, heads * 3 * HD), lambda s, p: (s, 0, p)),
        out_shape=jax.ShapeDtypeStruct((seqs, length, columns), jnp.bfloat16),
        scratch_shapes=[
            pltpu.VMEM((length, HD), jnp.float32),
            pltpu.VMEM((length, HD), jnp.float32),
        ],
        compiler_params=pltpu.CompilerParams(vmem_limit_bytes=VMEM),
        cost_estimate=pl.CostEstimate(
            flops=seqs * heads_here * length * length * HD * 20,
            bytes_accessed=seqs * length * columns * 6,
            transcendentals=seqs * heads_here * length * length,
        ),
    )(doc_starts, slopes, mixed, grad, sums)


def per_device(
    hidden_in,
    lengths,
    ln1_gain,
    ln1_bias,
    qkv_weight,
    qv_bias,
    dense_weight,
    dense_bias,
    ln2_gain,
    ln2_bias,
    fc1_weight,
    fc1_bias,
    fc2_weight,
    fc2_bias,
    cotangent,
):
    seqs_here, local_len, width = hidden_in.shape
    token_rows = seqs_here * local_len
    seq_ranks = lax.axis_size("seq")
    seq_length = local_len * seq_ranks
    heads_here = H // seq_ranks
    columns = heads_here * 3 * HD
    fsdp_ranks = lax.axis_size("fsdp")
    fsdp_rank = lax.axis_index("fsdp")

    small = [ln1_gain, ln1_bias, qv_bias, dense_bias, ln2_gain, ln2_bias, fc1_bias, fc2_bias]
    gathered = lax.all_gather(jnp.concatenate(small), "fsdp", axis=0).astype(jnp.float32)
    vectors, place = [], 0
    for part in small:
        size = part.shape[0]
        vectors.append(gathered[:, place : place + size].reshape(-1))
        place += size
    gain_one, shift_one, pair_bias, bias_dense, gain_two, shift_two, bias_up, bias_down = vectors

    head_columns = lax.dynamic_slice_in_dim(
        qkv_weight, lax.axis_index("seq") * columns, columns, 1
    )
    w_mixed = lax.all_gather(head_columns, "fsdp", axis=0, tiled=True)
    w_dense = lax.all_gather(dense_weight, "fsdp", axis=0, tiled=True)
    w_up = lax.all_gather(fc1_weight, "fsdp", axis=0, tiled=True)
    w_down = lax.all_gather(fc2_weight, "fsdp", axis=0, tiled=True)

    hidden_all = jnp.moveaxis(gather(hidden_in, "seq"), 0, 1).reshape(-1, width)
    normed = norm_layer(hidden_all.astype(jnp.float32), gain_one, shift_one).astype(jnp.bfloat16)
    mixed = (
        jnp.dot(normed, w_mixed, preferred_element_type=jnp.float32)
        + local_columns(pair_bias, heads_here)
    ).astype(jnp.bfloat16)
    mixed = mixed.reshape(seqs_here, seq_length, columns)
    head_ids = lax.axis_index("seq") * heads_here + jnp.arange(heads_here, dtype=jnp.int32)
    slopes = 2.0 ** (-8.0 * (head_ids + 1).astype(jnp.float32) / H)
    doc_starts = doc_starts_of(lengths, seq_length)
    attended_heads, log_sums = attend_forward(mixed, doc_starts, slopes)
    attended = lax.all_to_all(
        attended_heads, "seq", split_axis=1, concat_axis=2, tiled=True
    ).reshape(token_rows, width)

    tokens = hidden_in.reshape(token_rows, width).astype(jnp.float32)
    hidden = tokens + jnp.dot(attended, w_dense, preferred_element_type=jnp.float32) + bias_dense
    normed_two_f, norm_pull_two = jax.vjp(norm_layer, hidden, gain_two, shift_two)
    normed_two = normed_two_f.astype(jnp.bfloat16)
    activation = jnp.dot(normed_two, w_up, preferred_element_type=jnp.float32) + bias_up
    gelu_f, gelu_pull = jax.vjp(gelu_tanh, activation)
    gelu_out = gelu_f.astype(jnp.bfloat16)
    grad_out = cotangent.reshape(token_rows, width)
    grad_out_f = grad_out.astype(jnp.float32)

    core_first = labels_of("fsdp")[:1]
    far = labels_of("fsdp")[1:]
    g_w_down = contract_rows(gelu_out, grad_out).astype(jnp.bfloat16)
    g_w_down = reduce_rows(
        g_w_down, core_first + far + labels_of("seq", "dp"), ("fsdp", "seq", "dp")
    )
    result = hidden + jnp.dot(gelu_out, w_down, preferred_element_type=jnp.float32) + bias_down
    output = result.astype(jnp.bfloat16).reshape(seqs_here, local_len, width)

    g_bias_down = jnp.sum(grad_out_f, axis=0)
    grad_gelu = contract_cols(grad_out, w_down)
    grad_act = gelu_pull(grad_gelu)[0]
    g_bias_up = jnp.sum(grad_act, axis=0)
    grad_act_low = grad_act.astype(jnp.bfloat16)
    g_w_up = contract_rows(normed_two, grad_act_low).astype(jnp.bfloat16)
    g_w_up = reduce_rows(
        g_w_up, core_first + labels_of("seq") + far + labels_of("dp"), ("fsdp", "seq", "dp")
    )
    grad_normed_two = contract_cols(grad_act_low, w_up)
    grad_hidden_norm, g_gain_two, g_shift_two = norm_pull_two(grad_normed_two)
    grad_hidden = grad_out_f + grad_hidden_norm
    g_bias_dense = jnp.sum(grad_hidden, axis=0)
    grad_hidden_low = grad_hidden.astype(jnp.bfloat16)
    grad_attended = contract_cols(grad_hidden_low, w_dense).astype(jnp.bfloat16)
    grad_heads = lax.all_to_all(
        grad_attended.reshape(seqs_here, local_len, width),
        "seq",
        split_axis=2,
        concat_axis=1,
        tiled=True,
    )
    g_w_dense = contract_rows(attended, grad_hidden_low).astype(jnp.bfloat16)
    g_w_dense = reduce_rows(
        g_w_dense, core_first + far + labels_of("seq", "dp"), ("fsdp", "seq", "dp")
    )
    early = sum_all(
        pack([g_gain_two, g_shift_two, g_bias_up, g_bias_down, g_bias_dense]),
        ("fsdp", "seq", "dp"),
    ).reshape(-1)

    grad_mixed = attend_backward(mixed, grad_heads, log_sums, doc_starts, slopes)
    grad_mixed = grad_mixed.reshape(-1, columns)
    partial = contract_cols(grad_mixed, w_mixed).astype(jnp.bfloat16)
    seq_labels = [("seq", step) for step in reversed(steps_of("seq"))]
    partial = partial.reshape((seqs_here,) + (2,) * len(seq_labels) + (local_len, width))
    for label in list(seq_labels):
        partial = halve(partial, label[0], label[1], 1)
    g_w_mixed = contract_rows(normed, grad_mixed).astype(jnp.bfloat16)
    g_w_mixed = reduce_rows(g_w_mixed, core_first + far + labels_of("dp"), ("fsdp", "dp"))
    grad_normed = partial.reshape(token_rows, width).astype(jnp.float32)
    norm_pull_one = jax.vjp(norm_layer, tokens, gain_one, shift_one)[1]
    grad_token_norm, g_gain_one, g_shift_one = norm_pull_one(grad_normed)
    grad_input = (
        (grad_hidden + grad_token_norm)
        .astype(jnp.bfloat16)
        .reshape(seqs_here, local_len, width)
    )
    bias_total = jnp.sum(grad_mixed, axis=0, dtype=jnp.float32).reshape(heads_here, 3, HD)
    pair_total = jnp.concatenate([bias_total[:, :1], bias_total[:, 2:]], axis=1)
    g_pair_bias = lax.dynamic_update_slice_in_dim(
        jnp.zeros((H, 2, HD), jnp.float32), pair_total, lax.axis_index("seq") * heads_here, 0
    ).reshape(2 * H * HD)
    late = sum_all(pack([g_gain_one, g_shift_one, g_pair_bias]), ("fsdp", "seq", "dp"))
    late = late.reshape(-1)

    def own(packed, start, size):
        here = size // fsdp_ranks
        return lax.dynamic_slice_in_dim(packed, start + fsdp_rank * here, here, 0)

    hidden_units = bias_up.shape[0]
    g_gain_two = own(early, 0, width)
    g_shift_two = own(early, width, width)
    g_bias_up = own(early, 2 * width, hidden_units)
    g_bias_down = own(early, 2 * width + hidden_units, width)
    g_bias_dense = own(early, 3 * width + hidden_units, width)
    g_gain_one = own(late, 0, width)
    g_shift_one = own(late, width, width)
    g_pair_bias = own(late, 2 * width, 2 * H * HD)

    g_w_down = spread_rows(g_w_down, ("seq", "dp")).astype(jnp.float32)
    g_w_up = spread_rows(g_w_up, ("seq", "dp")).astype(jnp.float32)
    g_w_dense = spread_rows(g_w_dense, ("seq", "dp")).astype(jnp.float32)
    g_w_mixed = spread_rows(g_w_mixed, ("dp",))
    g_w_mixed = jnp.moveaxis(gather(g_w_mixed, "seq"), 0, 1).astype(jnp.float32)
    g_w_mixed = g_w_mixed.reshape(-1, seq_ranks * columns)
    return (
        output,
        grad_input,
        g_gain_one,
        g_shift_one,
        g_w_mixed,
        g_pair_bias,
        g_w_dense,
        g_bias_dense,
        g_gain_two,
        g_shift_two,
        g_w_up,
        g_bias_up,
        g_w_down,
        g_bias_down,
    )


def solution(mesh):
    placed = (
        P(("dp", "fsdp"), "seq", None),
        P(("dp", "fsdp"), None),
        P("fsdp"),
        P("fsdp"),
        P("fsdp", None),
        P("fsdp"),
        P("fsdp", None),
        P("fsdp"),
        P("fsdp"),
        P("fsdp"),
        P("fsdp", None),
        P("fsdp"),
        P("fsdp", None),
        P("fsdp"),
        P(("dp", "fsdp"), "seq", None),
    )
    return jax.shard_map(
        per_device,
        mesh=mesh,
        in_specs=placed,
        out_specs=(
            P(("dp", "fsdp"), "seq", None),
            P(("dp", "fsdp"), "seq", None),
            P("fsdp"),
            P("fsdp"),
            P("fsdp", None),
            P("fsdp"),
            P("fsdp", None),
            P("fsdp"),
            P("fsdp"),
            P("fsdp"),
            P("fsdp", None),
            P("fsdp"),
            P("fsdp", None),
            P("fsdp"),
        ),
        check_vma=False,
    )
```

```python
import functools
import math

import jax
import jax.numpy as jnp
from jax import lax
from jax.experimental import pallas as pl
from jax.experimental.pallas import tpu as pltpu
from jax.sharding import PartitionSpec as P

H = 16
HD = 64
ROWS = 256
VMEM = 48 * 1024 * 1024


EPSILON = 1e-05
GELU_COEF = 0.7978845608028654


def norm_layer(values, gain_vec, shift_vec):
    row_mean = jnp.mean(values, axis=-1, keepdims=True)
    centered = values - row_mean
    variance = jnp.mean(centered * centered, axis=-1, keepdims=True)
    return centered * lax.rsqrt(variance + EPSILON) * gain_vec + shift_vec


def gelu_tanh(values):
    return (
        0.5 * values * (1.0 + jnp.tanh(GELU_COEF * (values + 0.044715 * values * values * values)))
    )


def contract_rows(left_side, right_side):
    return lax.dot_general(
        left_side, right_side, (((0,), (0,)), ((), ())), preferred_element_type=jnp.float32
    )


def contract_cols(left_side, right_side):
    return lax.dot_general(
        left_side, right_side, (((1,), (1,)), ((), ())), preferred_element_type=jnp.float32
    )


def steps_of(axis):
    size = lax.axis_size(axis)
    return [2**k for k in range(size.bit_length() - 1)]


def bit_of(axis, step):
    return lax.rem(lax.axis_index(axis) // step, 2)


def swap(value, axis, step):
    pairs = [(i, i ^ step) for i in range(lax.axis_size(axis))]
    return lax.ppermute(value, axis, pairs)


def pick(value, dim, index):
    return lax.dynamic_index_in_dim(value, index, dim, keepdims=False)


class Order:
    def __init__(self, first):
        self.last = first

    def __call__(self, value):
        value, self.last = lax.optimization_barrier((value, self.last))
        return value


def double(value, axis, step, dim):
    other = swap(value, axis, step)
    first = jnp.stack([value, other], axis=dim)
    second = jnp.stack([other, value], axis=dim)
    return jnp.where(bit_of(axis, step) == 0, first, second)


def gather(value, axis):
    shape = value.shape
    value = value[None]
    for step in steps_of(axis):
        value = double(value, axis, step, 0).reshape((-1,) + shape)
    return value


def labels_of(*axes):
    return [(axis, step) for axis in axes for step in steps_of(axis)]


class Stage:
    def __init__(self, value):
        self.value = value


def halves(value, order, labels, groups):
    for group in groups:
        for place, (axis, step) in enumerate(group):
            dim = labels.index((axis, step))
            bit = bit_of(axis, step)
            received = swap(pick(value, dim, 1 - bit), axis, step)
            if place == 0:
                yield Stage(value)
            received = order(received)
            kept = pick(value, dim, bit).astype(jnp.float32)
            value = order((kept + received.astype(jnp.float32)).astype(jnp.bfloat16))
            labels.remove((axis, step))
    yield value


def sum_rows(grad, order, axes, groups, spread):
    labels = [(axis, step) for axis in axes for step in reversed(steps_of(axis))]
    columns = grad.shape[1]
    value = grad.reshape((2,) * len(labels) + (-1, columns))
    for value in halves(value, order, labels, groups):
        if isinstance(value, Stage):
            yield value
    for axis in reversed(spread):
        for place, step in enumerate(reversed(steps_of(axis))):
            other = swap(value, axis, step)
            if place == 0 or axis == "dp":
                yield Stage(value)
            other = order(other)
            first = jnp.stack([value, other], axis=place)
            second = jnp.stack([other, value], axis=place)
            value = order(jnp.where(bit_of(axis, step) == 0, first, second))
        value = value.reshape(-1, columns)
    yield value


def sum_all(value, order, axes):
    for axis, step in labels_of(*axes):
        received = swap(value, axis, step)
        yield Stage(value)
        value = order(value + order(received))
    yield value


def finish(chain):
    for value in chain:
        if not isinstance(value, Stage):
            return value


def doc_starts_of(lengths, seq_length):
    ends = jnp.cumsum(lengths, axis=1)
    positions = jnp.arange(seq_length, dtype=jnp.int32)
    passed = ends[:, :, None] <= positions[None, None, :]
    return jnp.max(jnp.where(passed, ends[:, :, None], 0), axis=1, keepdims=True)


def local_columns(pair_bias, heads_here):
    first = lax.axis_index("seq") * heads_here
    grouped = lax.dynamic_slice_in_dim(pair_bias.reshape(H, 2, HD), first, heads_here, 0)
    zeros = jnp.zeros((heads_here, 1, HD), grouped.dtype)
    stacked = jnp.concatenate([grouped[:, :1], zeros, grouped[:, 1:]], axis=1)
    return stacked.reshape(heads_here * 3 * HD)


def pack(parts):
    return jnp.concatenate(parts).reshape(-1, 128)


def attend_forward_kernel(*refs, block, heads):
    starts_ref, slopes_ref, mixed_ref = refs[:3]
    out_ref, sums_ref = refs[-2:]
    length = mixed_ref.shape[1]
    pair = pl.program_id(1)
    for head in range(heads):
        slope = slopes_ref[pair * heads + head]
        base = head * 3 * HD
        keys = mixed_ref[0, :, base + HD : base + 2 * HD]
        values_t = mixed_ref[0, :, base + 2 * HD : base + 3 * HD].T
        for start in range(0, length, block):
            stop = start + block
            query = mixed_ref[0, start:stop, base : base + HD] * jnp.bfloat16(1 / math.sqrt(HD))
            offsets = masked_offsets(starts_ref[0, :, start:stop], start, stop, block)
            scores = contract_cols(keys[:stop], query) + slope * offsets
            row_max = jnp.max(scores, axis=0, keepdims=True)
            terms = jnp.exp(scores - row_max)
            total = jnp.sum(terms, axis=0, keepdims=True)
            probs = (terms * (1.0 / total)).astype(jnp.bfloat16)
            attended = jnp.dot(
                values_t[:, :stop], probs, preferred_element_type=jnp.float32
            )
            out_ref[0, start:stop, head * HD : (head + 1) * HD] = attended.T.astype(jnp.bfloat16)
            sums_ref[0, 0, head : head + 1, start:stop] = row_max + jnp.log(total)


def masked_offsets(doc_starts, start, stop, block):
    key_pos = lax.broadcasted_iota(jnp.int32, (stop, block), 0)
    query_pos = lax.broadcasted_iota(jnp.int32, (stop, block), 1) + start
    allowed = (key_pos <= query_pos) & (key_pos >= doc_starts)
    return jnp.where(allowed, (key_pos - query_pos).astype(jnp.float32), -1e32)


def attend_backward_kernel(*refs, block, heads):
    starts_ref, slopes_ref, mixed_ref, grad_ref, sums_ref = refs[:5]
    out_ref, keys_acc, values_acc = refs[-3:]
    length = mixed_ref.shape[1]
    pair = pl.program_id(1)
    scale = 1 / math.sqrt(HD)
    for head in range(heads):
        slope = slopes_ref[pair * heads + head]
        base = head * 3 * HD
        keys = mixed_ref[0, :, base + HD : base + 2 * HD]
        keys_t = keys.T
        values = mixed_ref[0, :, base + 2 * HD : base + 3 * HD]
        for start in reversed(range(0, length, block)):
            stop = start + block
            query = mixed_ref[0, start:stop, base : base + HD] * jnp.bfloat16(scale)
            grad = grad_ref[0, start:stop, head * HD : (head + 1) * HD]
            offsets = masked_offsets(starts_ref[0, :, start:stop], start, stop, block)
            scores = contract_cols(keys[:stop], query) + slope * offsets
            probs = jnp.exp(scores - sums_ref[0, 0, head : head + 1, start:stop])
            grad_probs = contract_cols(values[:stop], grad)
            inner = jnp.sum(grad_probs * probs, axis=0, keepdims=True)
            grad_scores = (probs * (grad_probs - inner)).astype(jnp.bfloat16)
            grad_query = jnp.dot(
                keys_t[:, :stop], grad_scores, preferred_element_type=jnp.float32
            )
            out_ref[0, start:stop, base : base + HD] = (grad_query.T * scale).astype(jnp.bfloat16)
            grad_keys = jnp.dot(grad_scores, query, preferred_element_type=jnp.float32)
            grad_values = jnp.dot(
                probs.astype(jnp.bfloat16), grad, preferred_element_type=jnp.float32
            )
            if stop == length:
                keys_acc[...] = grad_keys
                values_acc[...] = grad_values
            else:
                keys_acc[:stop] += grad_keys
                values_acc[:stop] += grad_values
        out_ref[0, :, base + HD : base + 2 * HD] = keys_acc[...].astype(jnp.bfloat16)
        out_ref[0, :, base + 2 * HD : base + 3 * HD] = values_acc[...].astype(jnp.bfloat16)


def attention_specs(length, heads):
    return [
        pl.BlockSpec((1, 1, length), lambda s, p: (s, 0, 0)),
        pl.BlockSpec(memory_space=pltpu.SMEM),
        pl.BlockSpec((1, length, heads * 3 * HD), lambda s, p: (s, 0, p)),
    ]


def attend_forward(mixed, doc_starts, slopes, ahead):
    seqs, length, columns = mixed.shape
    heads_here = columns // (3 * HD)
    heads = min(2, heads_here)
    pairs = heads_here // heads
    return pl.pallas_call(
        functools.partial(attend_forward_kernel, block=min(ROWS, length), heads=heads),
        grid=(seqs, pairs),
        in_specs=attention_specs(length, heads)
        + [pl.BlockSpec(memory_space=pl.ANY)] * len(ahead),
        out_specs=[
            pl.BlockSpec((1, length, heads * HD), lambda s, p: (s, 0, p)),
            pl.BlockSpec((1, 1, heads, length), lambda s, p: (s, p, 0, 0)),
        ],
        out_shape=[
            jax.ShapeDtypeStruct((seqs, length, heads_here * HD), jnp.bfloat16),
            jax.ShapeDtypeStruct((seqs, pairs, heads, length), jnp.float32),
        ],
        compiler_params=pltpu.CompilerParams(vmem_limit_bytes=VMEM),
        cost_estimate=pl.CostEstimate(
            flops=seqs * heads_here * length * length * HD * 8,
            bytes_accessed=seqs * length * columns * 4,
            transcendentals=seqs * heads_here * length * length,
        ),
    )(doc_starts, slopes, mixed, *ahead)


def attend_backward(mixed, grad, sums, doc_starts, slopes, ahead):
    seqs, length, columns = mixed.shape
    heads_here = columns // (3 * HD)
    heads = min(2, heads_here)
    pairs = heads_here // heads
    return pl.pallas_call(
        functools.partial(attend_backward_kernel, block=min(ROWS, length), heads=heads),
        grid=(seqs, pairs),
        in_specs=attention_specs(length, heads)
        + [
            pl.BlockSpec((1, length, heads * HD), lambda s, p: (s, 0, p)),
            pl.BlockSpec((1, 1, heads, length), lambda s, p: (s, p, 0, 0)),
        ]
        + [pl.BlockSpec(memory_space=pl.ANY)] * len(ahead),
        out_specs=pl.BlockSpec((1, length, heads * 3 * HD), lambda s, p: (s, 0, p)),
        out_shape=jax.ShapeDtypeStruct((seqs, length, columns), jnp.bfloat16),
        scratch_shapes=[
            pltpu.VMEM((length, HD), jnp.float32),
            pltpu.VMEM((length, HD), jnp.float32),
        ],
        compiler_params=pltpu.CompilerParams(vmem_limit_bytes=VMEM),
        cost_estimate=pl.CostEstimate(
            flops=seqs * heads_here * length * length * HD * 20,
            bytes_accessed=seqs * length * columns * 6,
            transcendentals=seqs * heads_here * length * length,
        ),
    )(doc_starts, slopes, mixed, grad, sums, *ahead)


def per_device(
    hidden_in,
    lengths,
    ln1_gain,
    ln1_bias,
    qkv_weight,
    qv_bias,
    dense_weight,
    dense_bias,
    ln2_gain,
    ln2_bias,
    fc1_weight,
    fc1_bias,
    fc2_weight,
    fc2_bias,
    cotangent,
):
    seqs_here, local_len, width = hidden_in.shape
    token_rows = seqs_here * local_len
    seq_ranks = lax.axis_size("seq")
    seq_length = local_len * seq_ranks
    heads_here = H // seq_ranks
    columns = heads_here * 3 * HD
    fsdp_ranks = lax.axis_size("fsdp")
    fsdp_rank = lax.axis_index("fsdp")

    small = [ln1_gain, ln1_bias, qv_bias, dense_bias, ln2_gain, ln2_bias, fc1_bias, fc2_bias]
    gathered = lax.all_gather(jnp.concatenate(small), "fsdp", axis=0).astype(jnp.float32)
    vectors, place = [], 0
    for part in small:
        size = part.shape[0]
        vectors.append(gathered[:, place : place + size].reshape(-1))
        place += size
    gain_one, shift_one, pair_bias, bias_dense, gain_two, shift_two, bias_up, bias_down = vectors

    head_columns = lax.dynamic_slice_in_dim(
        qkv_weight, lax.axis_index("seq") * columns, columns, 1
    )
    w_mixed = lax.all_gather(head_columns, "fsdp", axis=0, tiled=True)
    w_dense = lax.all_gather(dense_weight, "fsdp", axis=0, tiled=True)
    w_up = lax.all_gather(fc1_weight, "fsdp", axis=0, tiled=True)
    split_down = fsdp_ranks == 4 and seq_ranks == 2
    ahead = []
    if split_down:
        half = fc2_weight.reshape(2, -1, width)
        far_half = swap(pick(half, 0, lax.axis_index("seq")), "fsdp", 2)
        ahead = [far_half]
        far_shard = double(far_half, "seq", 1, 0).reshape(fc2_weight.shape)
        near = bit_of("fsdp", 2) == 0
        shards = jnp.where(
            near, jnp.stack([fc2_weight, far_shard]), jnp.stack([far_shard, fc2_weight])
        )
        w_down = double(shards, "fsdp", 1, 1).reshape(-1, width)
    else:
        w_down = lax.all_gather(fc2_weight, "fsdp", axis=0, tiled=True)

    hidden_all = jnp.moveaxis(gather(hidden_in, "seq"), 0, 1).reshape(-1, width)
    normed = norm_layer(hidden_all.astype(jnp.float32), gain_one, shift_one).astype(jnp.bfloat16)
    mixed = (
        jnp.dot(normed, w_mixed, preferred_element_type=jnp.float32)
        + local_columns(pair_bias, heads_here)
    ).astype(jnp.bfloat16)
    mixed = mixed.reshape(seqs_here, seq_length, columns)
    head_ids = lax.axis_index("seq") * heads_here + jnp.arange(heads_here, dtype=jnp.int32)
    slopes = 2.0 ** (-8.0 * (head_ids + 1).astype(jnp.float32) / H)
    doc_starts = doc_starts_of(lengths, seq_length)
    attended_heads, log_sums = attend_forward(mixed, doc_starts, slopes, ahead)
    attended = lax.all_to_all(
        attended_heads, "seq", split_axis=1, concat_axis=2, tiled=True
    ).reshape(token_rows, width)

    tokens = hidden_in.reshape(token_rows, width).astype(jnp.float32)
    hidden = tokens + jnp.dot(attended, w_dense, preferred_element_type=jnp.float32) + bias_dense
    normed_two_f, norm_pull_two = jax.vjp(norm_layer, hidden, gain_two, shift_two)
    normed_two = normed_two_f.astype(jnp.bfloat16)
    activation = jnp.dot(normed_two, w_up, preferred_element_type=jnp.float32) + bias_up
    gelu_f, gelu_pull = jax.vjp(gelu_tanh, activation)
    gelu_out = gelu_f.astype(jnp.bfloat16)
    grad_out = cotangent.reshape(token_rows, width)
    grad_out_f = grad_out.astype(jnp.float32)

    core = labels_of("fsdp")[:1]
    far = labels_of("fsdp")[1:]
    ranks = labels_of("seq")
    near_z, far_z = labels_of("dp")[:1], labels_of("dp")[1:]
    every = ("fsdp", "seq", "dp")
    order = Order(gelu_out)

    g_w_down = order(contract_rows(gelu_out, grad_out).astype(jnp.bfloat16))
    down = sum_rows(g_w_down, order, every, [core, far, ranks, near_z, far_z], ("seq", "dp"))
    next(down)
    next(down)
    w_down = order(w_down)
    grad_gelu = contract_cols(grad_out, w_down)
    grad_act = gelu_pull(grad_gelu)[0]
    g_bias_up = jnp.sum(grad_act, axis=0)
    grad_act_low = order(grad_act.astype(jnp.bfloat16))
    g_w_up = order(contract_rows(normed_two, grad_act_low).astype(jnp.bfloat16))
    up = sum_rows(g_w_up, order, every, [core, ranks, far, near_z, far_z], ("seq", "dp"))
    next(up)
    grad_normed_two = order(contract_cols(grad_act_low, w_up))
    grad_hidden_norm, g_gain_two, g_shift_two = norm_pull_two(grad_normed_two)
    grad_hidden = grad_out_f + grad_hidden_norm
    grad_hidden_low = grad_hidden.astype(jnp.bfloat16)
    grad_attended = order(contract_cols(grad_hidden_low, w_dense).astype(jnp.bfloat16))
    grad_heads = order(
        lax.all_to_all(
            grad_attended.reshape(seqs_here, local_len, width),
            "seq",
            split_axis=2,
            concat_axis=1,
            tiled=True,
        )
    )
    ahead = [next(up).value]
    g_w_dense = order(contract_rows(attended, grad_hidden_low).astype(jnp.bfloat16))
    dense = sum_rows(g_w_dense, order, every, [core, far, ranks, near_z, far_z], ("seq", "dp"))
    next(dense)
    ahead += [next(down).value, next(dense).value]

    grad_mixed = order(
        attend_backward(mixed, grad_heads, log_sums, doc_starts, slopes, ahead)
    )
    grad_mixed = grad_mixed.reshape(-1, columns)
    partial = order(contract_cols(grad_mixed, w_mixed).astype(jnp.bfloat16))
    seq_labels = [("seq", step) for step in reversed(steps_of("seq"))]
    partial = partial.reshape((seqs_here,) + (2,) * len(seq_labels) + (local_len, width))
    partial = jnp.moveaxis(partial, 0, len(seq_labels))
    token_sums = halves(partial, order, list(seq_labels), [ranks])
    next(token_sums)
    g_w_mixed = order(contract_rows(normed, grad_mixed).astype(jnp.bfloat16))
    qkv = sum_rows(g_w_mixed, order, ("fsdp", "dp"), [core, far, near_z, far_z], ("dp",))
    next(qkv)
    next(up)
    next(down)
    next(qkv)
    grad_normed = finish(token_sums).reshape(token_rows, width).astype(jnp.float32)
    norm_pull_one = jax.vjp(norm_layer, tokens, gain_one, shift_one)[1]
    grad_token_norm, g_gain_one, g_shift_one = norm_pull_one(grad_normed)
    grad_input = (
        (grad_hidden + grad_token_norm)
        .astype(jnp.bfloat16)
        .reshape(seqs_here, local_len, width)
    )
    next(down)
    g_bias_down = jnp.sum(grad_out_f, axis=0)
    g_bias_dense = jnp.sum(grad_hidden, axis=0)
    bias_total = jnp.sum(grad_mixed, axis=0, dtype=jnp.float32).reshape(heads_here, 3, HD)
    pair_total = jnp.concatenate([bias_total[:, :1], bias_total[:, 2:]], axis=1)
    g_pair_bias = lax.dynamic_update_slice_in_dim(
        jnp.zeros((H, 2, HD), jnp.float32), pair_total, lax.axis_index("seq") * heads_here, 0
    ).reshape(2 * H * HD)
    packed = pack(
        [
            g_gain_two,
            g_shift_two,
            g_bias_up,
            g_bias_down,
            g_bias_dense,
            g_gain_one,
            g_shift_one,
            g_pair_bias,
        ]
    )
    vector_sums = sum_all(order(packed), order, every)
    next(vector_sums)
    next(dense)
    next(down)
    next(vector_sums)
    next(up)
    next(qkv)
    next(vector_sums)
    next(down)
    next(dense)
    result = hidden + jnp.dot(gelu_out, w_down, preferred_element_type=jnp.float32) + bias_down
    output = order(result.astype(jnp.bfloat16)).reshape(seqs_here, local_len, width)
    next(vector_sums)
    next(up)
    next(qkv)
    next(dense)
    next(vector_sums)
    next(up)
    next(qkv)
    next(dense)
    next(up)
    next(qkv)
    next(dense)
    g_w_down = finish(down).astype(jnp.float32)
    small_sums = finish(vector_sums).reshape(-1)
    next(up)
    g_w_mixed = finish(qkv)
    g_w_mixed = gather(g_w_mixed, "seq")
    next(dense)
    g_w_up = finish(up).astype(jnp.float32)
    g_w_dense = finish(dense).astype(jnp.float32)
    g_w_mixed = jnp.moveaxis(g_w_mixed, 0, 1).astype(jnp.float32)
    g_w_mixed = g_w_mixed.reshape(-1, seq_ranks * columns)

    def own(packed, start, size):
        here = size // fsdp_ranks
        return lax.dynamic_slice_in_dim(packed, start + fsdp_rank * here, here, 0)

    hidden_units = bias_up.shape[0]
    g_gain_two = own(small_sums, 0, width)
    g_shift_two = own(small_sums, width, width)
    g_bias_up = own(small_sums, 2 * width, hidden_units)
    g_bias_down = own(small_sums, 2 * width + hidden_units, width)
    g_bias_dense = own(small_sums, 3 * width + hidden_units, width)
    g_gain_one = own(small_sums, 4 * width + hidden_units, width)
    g_shift_one = own(small_sums, 5 * width + hidden_units, width)
    g_pair_bias = own(small_sums, 6 * width + hidden_units, 2 * H * HD)

    return (
        output,
        grad_input,
        g_gain_one,
        g_shift_one,
        g_w_mixed,
        g_pair_bias,
        g_w_dense,
        g_bias_dense,
        g_gain_two,
        g_shift_two,
        g_w_up,
        g_bias_up,
        g_w_down,
        g_bias_down,
    )


def solution(mesh):
    placed = (
        P(("dp", "fsdp"), "seq", None),
        P(("dp", "fsdp"), None),
        P("fsdp"),
        P("fsdp"),
        P("fsdp", None),
        P("fsdp"),
        P("fsdp", None),
        P("fsdp"),
        P("fsdp"),
        P("fsdp"),
        P("fsdp", None),
        P("fsdp"),
        P("fsdp", None),
        P("fsdp"),
        P(("dp", "fsdp"), "seq", None),
    )
    return jax.shard_map(
        per_device,
        mesh=mesh,
        in_specs=placed,
        out_specs=(
            P(("dp", "fsdp"), "seq", None),
            P(("dp", "fsdp"), "seq", None),
            P("fsdp"),
            P("fsdp"),
            P("fsdp", None),
            P("fsdp"),
            P("fsdp", None),
            P("fsdp"),
            P("fsdp"),
            P("fsdp"),
            P("fsdp", None),
            P("fsdp"),
            P("fsdp", None),
            P("fsdp"),
        ),
        check_vma=False,
    )
```

```python
import functools
import math

import jax
import jax.numpy as jnp
from jax import lax
from jax.experimental import pallas as pl
from jax.experimental.pallas import tpu as pltpu
from jax.sharding import PartitionSpec as P

H = 16
HD = 64
ROWS = 256
VMEM = 48 * 1024 * 1024


EPSILON = 1e-05
GELU_COEF = 0.7978845608028654


def norm_layer(values, gain_vec, shift_vec):
    row_mean = jnp.mean(values, axis=-1, keepdims=True)
    centered = values - row_mean
    variance = jnp.mean(centered * centered, axis=-1, keepdims=True)
    return centered * lax.rsqrt(variance + EPSILON) * gain_vec + shift_vec


def gelu_tanh(values):
    return (
        0.5 * values * (1.0 + jnp.tanh(GELU_COEF * (values + 0.044715 * values * values * values)))
    )


def contract_rows(left_side, right_side):
    return lax.dot_general(
        left_side, right_side, (((0,), (0,)), ((), ())), preferred_element_type=jnp.float32
    )


def contract_cols(left_side, right_side):
    return lax.dot_general(
        left_side, right_side, (((1,), (1,)), ((), ())), preferred_element_type=jnp.float32
    )


def steps_of(axis):
    size = lax.axis_size(axis)
    return [2**k for k in range(size.bit_length() - 1)]


def bit_of(axis, step):
    return lax.rem(lax.axis_index(axis) // step, 2)


def swap(value, axis, step):
    pairs = [(i, i ^ step) for i in range(lax.axis_size(axis))]
    return lax.ppermute(value, axis, pairs)


def pick(value, dim, index):
    return lax.dynamic_index_in_dim(value, index, dim, keepdims=False)


class Order:
    def __init__(self, first):
        self.last = first

    def __call__(self, value):
        value, self.last = lax.optimization_barrier((value, self.last))
        return value


def double(value, axis, step, dim):
    other = swap(value, axis, step)
    first = jnp.stack([value, other], axis=dim)
    second = jnp.stack([other, value], axis=dim)
    return jnp.where(bit_of(axis, step) == 0, first, second)


def gather(value, axis):
    shape = value.shape
    value = value[None]
    for step in steps_of(axis):
        value = double(value, axis, step, 0).reshape((-1,) + shape)
    return value


def labels_of(*axes):
    return [(axis, step) for axis in axes for step in steps_of(axis)]


class Stage:
    def __init__(self, value):
        self.value = value


def halves(value, order, labels, groups):
    for group in groups:
        for place, (axis, step) in enumerate(group):
            dim = labels.index((axis, step))
            bit = bit_of(axis, step)
            received = swap(pick(value, dim, 1 - bit), axis, step)
            if place == 0:
                yield Stage(value)
            received = order(received)
            kept = pick(value, dim, bit).astype(jnp.float32)
            value = order((kept + received.astype(jnp.float32)).astype(jnp.bfloat16))
            labels.remove((axis, step))
    yield value


def sum_rows(grad, order, axes, groups, spread):
    labels = [(axis, step) for axis in axes for step in reversed(steps_of(axis))]
    columns = grad.shape[1]
    value = grad.reshape((2,) * len(labels) + (-1, columns))
    for value in halves(value, order, labels, groups):
        if isinstance(value, Stage):
            yield value
    for axis in reversed(spread):
        for place, step in enumerate(reversed(steps_of(axis))):
            other = swap(value, axis, step)
            if place == 0 or axis == "dp":
                yield Stage(value)
            other = order(other)
            first = jnp.stack([value, other], axis=place)
            second = jnp.stack([other, value], axis=place)
            value = order(jnp.where(bit_of(axis, step) == 0, first, second))
        value = value.reshape(-1, columns)
    yield value


def sum_all(value, order, axes):
    for axis, step in labels_of(*axes):
        received = swap(value, axis, step)
        yield Stage(value)
        value = order(value + order(received))
    yield value


def finish(chain):
    for value in chain:
        if not isinstance(value, Stage):
            return value


def doc_starts_of(lengths, seq_length):
    ends = jnp.cumsum(lengths, axis=1)
    positions = jnp.arange(seq_length, dtype=jnp.int32)
    passed = ends[:, :, None] <= positions[None, None, :]
    return jnp.max(jnp.where(passed, ends[:, :, None], 0), axis=1, keepdims=True)


def local_columns(pair_bias, heads_here):
    first = lax.axis_index("seq") * heads_here
    grouped = lax.dynamic_slice_in_dim(pair_bias.reshape(H, 2, HD), first, heads_here, 0)
    zeros = jnp.zeros((heads_here, 1, HD), grouped.dtype)
    stacked = jnp.concatenate([grouped[:, :1], zeros, grouped[:, 1:]], axis=1)
    return stacked.reshape(heads_here * 3 * HD)


def pack(parts):
    return jnp.concatenate(parts).reshape(-1, 128)


def pass_on_kernel(*refs):
    refs[-1][...] = refs[0][...]


def after_arrays(vector, ahead):
    rows = vector.reshape(-1, 128)
    return pl.pallas_call(
        pass_on_kernel,
        in_specs=[pl.BlockSpec(memory_space=pltpu.VMEM)]
        + [pl.BlockSpec(memory_space=pl.ANY)] * len(ahead),
        out_specs=pl.BlockSpec(memory_space=pltpu.VMEM),
        out_shape=jax.ShapeDtypeStruct(rows.shape, rows.dtype),
    )(rows, *ahead).reshape(vector.shape)


def attend_forward_kernel(*refs, block, heads):
    starts_ref, slopes_ref, mixed_ref = refs[:3]
    out_ref, sums_ref = refs[-2:]
    length = mixed_ref.shape[1]
    pair = pl.program_id(1)
    for head in range(heads):
        slope = slopes_ref[pair * heads + head]
        base = head * 3 * HD
        keys = mixed_ref[0, :, base + HD : base + 2 * HD]
        values_t = mixed_ref[0, :, base + 2 * HD : base + 3 * HD].T
        for start in range(0, length, block):
            stop = start + block
            query = mixed_ref[0, start:stop, base : base + HD] * jnp.bfloat16(1 / math.sqrt(HD))
            offsets = masked_offsets(starts_ref[0, :, start:stop], start, stop, block)
            scores = contract_cols(keys[:stop], query) + slope * offsets
            row_max = jnp.max(scores, axis=0, keepdims=True)
            terms = jnp.exp(scores - row_max)
            total = jnp.sum(terms, axis=0, keepdims=True)
            probs = (terms * (1.0 / total)).astype(jnp.bfloat16)
            attended = jnp.dot(
                values_t[:, :stop], probs, preferred_element_type=jnp.float32
            )
            out_ref[0, start:stop, head * HD : (head + 1) * HD] = attended.T.astype(jnp.bfloat16)
            sums_ref[0, 0, head : head + 1, start:stop] = row_max + jnp.log(total)


def masked_offsets(doc_starts, start, stop, block):
    key_pos = lax.broadcasted_iota(jnp.int32, (stop, block), 0)
    query_pos = lax.broadcasted_iota(jnp.int32, (stop, block), 1) + start
    allowed = (key_pos <= query_pos) & (key_pos >= doc_starts)
    return jnp.where(allowed, (key_pos - query_pos).astype(jnp.float32), -1e32)


def attend_backward_kernel(*refs, block, heads):
    starts_ref, slopes_ref, mixed_ref, grad_ref, sums_ref = refs[:5]
    out_ref, keys_acc, values_acc = refs[-3:]
    length = mixed_ref.shape[1]
    pair = pl.program_id(1)
    scale = 1 / math.sqrt(HD)
    for head in range(heads):
        slope = slopes_ref[pair * heads + head]
        base = head * 3 * HD
        keys = mixed_ref[0, :, base + HD : base + 2 * HD]
        keys_t = keys.T
        values = mixed_ref[0, :, base + 2 * HD : base + 3 * HD]
        for start in reversed(range(0, length, block)):
            stop = start + block
            query = mixed_ref[0, start:stop, base : base + HD] * jnp.bfloat16(scale)
            grad = grad_ref[0, start:stop, head * HD : (head + 1) * HD]
            offsets = masked_offsets(starts_ref[0, :, start:stop], start, stop, block)
            scores = contract_cols(keys[:stop], query) + slope * offsets
            probs = jnp.exp(scores - sums_ref[0, 0, head : head + 1, start:stop])
            grad_probs = contract_cols(values[:stop], grad)
            inner = jnp.sum(grad_probs * probs, axis=0, keepdims=True)
            grad_scores = (probs * (grad_probs - inner)).astype(jnp.bfloat16)
            grad_query = jnp.dot(
                keys_t[:, :stop], grad_scores, preferred_element_type=jnp.float32
            )
            out_ref[0, start:stop, base : base + HD] = (grad_query.T * scale).astype(jnp.bfloat16)
            grad_keys = jnp.dot(grad_scores, query, preferred_element_type=jnp.float32)
            grad_values = jnp.dot(
                probs.astype(jnp.bfloat16), grad, preferred_element_type=jnp.float32
            )
            if stop == length:
                keys_acc[...] = grad_keys
                values_acc[...] = grad_values
            else:
                keys_acc[:stop] += grad_keys
                values_acc[:stop] += grad_values
        out_ref[0, :, base + HD : base + 2 * HD] = keys_acc[...].astype(jnp.bfloat16)
        out_ref[0, :, base + 2 * HD : base + 3 * HD] = values_acc[...].astype(jnp.bfloat16)


def attention_specs(length, heads):
    return [
        pl.BlockSpec((1, 1, length), lambda s, p: (s, 0, 0)),
        pl.BlockSpec(memory_space=pltpu.SMEM),
        pl.BlockSpec((1, length, heads * 3 * HD), lambda s, p: (s, 0, p)),
    ]


def attend_forward(mixed, doc_starts, slopes, ahead):
    seqs, length, columns = mixed.shape
    heads_here = columns // (3 * HD)
    heads = min(2, heads_here)
    pairs = heads_here // heads
    return pl.pallas_call(
        functools.partial(attend_forward_kernel, block=min(ROWS, length), heads=heads),
        grid=(seqs, pairs),
        in_specs=attention_specs(length, heads)
        + [pl.BlockSpec(memory_space=pl.ANY)] * len(ahead),
        out_specs=[
            pl.BlockSpec((1, length, heads * HD), lambda s, p: (s, 0, p)),
            pl.BlockSpec((1, 1, heads, length), lambda s, p: (s, p, 0, 0)),
        ],
        out_shape=[
            jax.ShapeDtypeStruct((seqs, length, heads_here * HD), jnp.bfloat16),
            jax.ShapeDtypeStruct((seqs, pairs, heads, length), jnp.float32),
        ],
        compiler_params=pltpu.CompilerParams(vmem_limit_bytes=VMEM),
        cost_estimate=pl.CostEstimate(
            flops=seqs * heads_here * length * length * HD * 8,
            bytes_accessed=seqs * length * columns * 4,
            transcendentals=seqs * heads_here * length * length,
        ),
    )(doc_starts, slopes, mixed, *ahead)


def attend_backward(mixed, grad, sums, doc_starts, slopes, ahead):
    seqs, length, columns = mixed.shape
    heads_here = columns // (3 * HD)
    heads = min(2, heads_here)
    pairs = heads_here // heads
    return pl.pallas_call(
        functools.partial(attend_backward_kernel, block=min(ROWS, length), heads=heads),
        grid=(seqs, pairs),
        in_specs=attention_specs(length, heads)
        + [
            pl.BlockSpec((1, length, heads * HD), lambda s, p: (s, 0, p)),
            pl.BlockSpec((1, 1, heads, length), lambda s, p: (s, p, 0, 0)),
        ]
        + [pl.BlockSpec(memory_space=pl.ANY)] * len(ahead),
        out_specs=pl.BlockSpec((1, length, heads * 3 * HD), lambda s, p: (s, 0, p)),
        out_shape=jax.ShapeDtypeStruct((seqs, length, columns), jnp.bfloat16),
        scratch_shapes=[
            pltpu.VMEM((length, HD), jnp.float32),
            pltpu.VMEM((length, HD), jnp.float32),
        ],
        compiler_params=pltpu.CompilerParams(vmem_limit_bytes=VMEM),
        cost_estimate=pl.CostEstimate(
            flops=seqs * heads_here * length * length * HD * 20,
            bytes_accessed=seqs * length * columns * 6,
            transcendentals=seqs * heads_here * length * length,
        ),
    )(doc_starts, slopes, mixed, grad, sums, *ahead)


def per_device(
    hidden_in,
    lengths,
    ln1_gain,
    ln1_bias,
    qkv_weight,
    qv_bias,
    dense_weight,
    dense_bias,
    ln2_gain,
    ln2_bias,
    fc1_weight,
    fc1_bias,
    fc2_weight,
    fc2_bias,
    cotangent,
):
    seqs_here, local_len, width = hidden_in.shape
    token_rows = seqs_here * local_len
    seq_ranks = lax.axis_size("seq")
    seq_length = local_len * seq_ranks
    heads_here = H // seq_ranks
    columns = heads_here * 3 * HD
    fsdp_ranks = lax.axis_size("fsdp")
    fsdp_rank = lax.axis_index("fsdp")

    small = [ln1_gain, ln1_bias, qv_bias, dense_bias, ln2_gain, ln2_bias, fc1_bias, fc2_bias]
    gathered = gather(jnp.concatenate(small), "fsdp").astype(jnp.float32)
    vectors, place = [], 0
    for part in small:
        size = part.shape[0]
        vectors.append(gathered[:, place : place + size].reshape(-1))
        place += size
    gain_one, shift_one, pair_bias, bias_dense, gain_two, shift_two, bias_up, bias_down = vectors

    head_columns = lax.dynamic_slice_in_dim(
        qkv_weight, lax.axis_index("seq") * columns, columns, 1
    )
    w_mixed = lax.all_gather(head_columns, "fsdp", axis=0, tiled=True)
    w_dense = lax.all_gather(dense_weight, "fsdp", axis=0, tiled=True)
    w_up = lax.all_gather(fc1_weight, "fsdp", axis=0, tiled=True)
    split_down = fsdp_ranks == 4 and seq_ranks == 2
    ahead = []
    if split_down:
        half = fc2_weight.reshape(2, -1, width)
        far_half = swap(pick(half, 0, lax.axis_index("seq")), "fsdp", 2)
        ahead = [far_half]
        far_shard = double(far_half, "seq", 1, 0).reshape(fc2_weight.shape)
        near = bit_of("fsdp", 2) == 0
        shards = jnp.where(
            near, jnp.stack([fc2_weight, far_shard]), jnp.stack([far_shard, fc2_weight])
        )
        w_down = double(shards, "fsdp", 1, 1).reshape(-1, width)
    else:
        w_down = lax.all_gather(fc2_weight, "fsdp", axis=0, tiled=True)

    hidden_all = jnp.moveaxis(gather(hidden_in, "seq"), 0, 1).reshape(-1, width)
    normed = norm_layer(hidden_all.astype(jnp.float32), gain_one, shift_one).astype(jnp.bfloat16)
    mixed = (
        jnp.dot(normed, w_mixed, preferred_element_type=jnp.float32)
        + local_columns(pair_bias, heads_here)
    ).astype(jnp.bfloat16)
    mixed = mixed.reshape(seqs_here, seq_length, columns)
    head_ids = lax.axis_index("seq") * heads_here + jnp.arange(heads_here, dtype=jnp.int32)
    slopes = 2.0 ** (-8.0 * (head_ids + 1).astype(jnp.float32) / H)
    doc_starts = doc_starts_of(lengths, seq_length)
    attended_heads, log_sums = attend_forward(mixed, doc_starts, slopes, ahead)
    attended = lax.all_to_all(
        attended_heads, "seq", split_axis=1, concat_axis=2, tiled=True
    ).reshape(token_rows, width)

    tokens = hidden_in.reshape(token_rows, width).astype(jnp.float32)
    hidden = tokens + jnp.dot(attended, w_dense, preferred_element_type=jnp.float32) + bias_dense
    normed_two = norm_layer(hidden, gain_two, shift_two).astype(jnp.bfloat16)
    activation = jnp.dot(normed_two, w_up, preferred_element_type=jnp.float32) + bias_up
    gelu_f, gelu_pull = jax.vjp(gelu_tanh, activation)
    gelu_out = gelu_f.astype(jnp.bfloat16)
    grad_out = cotangent.reshape(token_rows, width)
    grad_out_f = grad_out.astype(jnp.float32)

    core = labels_of("fsdp")[:1]
    far = labels_of("fsdp")[1:]
    ranks = labels_of("seq")
    near_z, far_z = labels_of("dp")[:1], labels_of("dp")[1:]
    every = ("fsdp", "seq", "dp")
    order = Order(gelu_out)

    g_w_down = order(contract_rows(gelu_out, grad_out).astype(jnp.bfloat16))
    down = sum_rows(g_w_down, order, every, [core, far, ranks, near_z, far_z], ("seq", "dp"))
    next(down)
    next(down)
    w_down = order(w_down)
    grad_gelu = contract_cols(grad_out, w_down)
    grad_act = gelu_pull(grad_gelu)[0]
    g_bias_up = jnp.sum(grad_act, axis=0)
    grad_act_low = order(grad_act.astype(jnp.bfloat16))
    g_w_up = order(contract_rows(normed_two, grad_act_low).astype(jnp.bfloat16))
    up = sum_rows(g_w_up, order, every, [core, ranks, far, near_z, far_z], ("seq", "dp"))
    next(up)
    grad_normed_two = order(contract_cols(grad_act_low, w_up))
    summed_down = next(down).value
    late_gain = after_arrays(gain_two, [summed_down])
    norm_pull_two = jax.vjp(norm_layer, hidden, late_gain, shift_two)[1]
    grad_hidden_norm, g_gain_two, g_shift_two = norm_pull_two(grad_normed_two)
    grad_hidden = grad_out_f + grad_hidden_norm
    grad_hidden_low = grad_hidden.astype(jnp.bfloat16)
    grad_attended = order(contract_cols(grad_hidden_low, w_dense).astype(jnp.bfloat16))
    grad_heads = order(
        lax.all_to_all(
            grad_attended.reshape(seqs_here, local_len, width),
            "seq",
            split_axis=2,
            concat_axis=1,
            tiled=True,
        )
    )
    ahead = [next(up).value]
    g_w_dense = order(contract_rows(attended, grad_hidden_low).astype(jnp.bfloat16))
    dense = sum_rows(g_w_dense, order, every, [core, far, ranks, near_z, far_z], ("seq", "dp"))
    next(dense)
    ahead += [summed_down, next(dense).value]

    grad_mixed = order(
        attend_backward(mixed, grad_heads, log_sums, doc_starts, slopes, ahead)
    )
    grad_mixed = grad_mixed.reshape(-1, columns)
    partial = order(contract_cols(grad_mixed, w_mixed).astype(jnp.bfloat16))
    seq_labels = [("seq", step) for step in reversed(steps_of("seq"))]
    partial = partial.reshape((seqs_here,) + (2,) * len(seq_labels) + (local_len, width))
    partial = jnp.moveaxis(partial, 0, len(seq_labels))
    token_sums = halves(partial, order, list(seq_labels), [ranks])
    next(token_sums)
    g_w_mixed = order(contract_rows(normed, grad_mixed).astype(jnp.bfloat16))
    qkv = sum_rows(g_w_mixed, order, ("fsdp", "dp"), [core, far, near_z, far_z], ("dp",))
    next(qkv)
    next(up)
    next(down)
    next(qkv)
    grad_normed = finish(token_sums).reshape(token_rows, width).astype(jnp.float32)
    norm_pull_one = jax.vjp(norm_layer, tokens, gain_one, shift_one)[1]
    grad_token_norm, g_gain_one, g_shift_one = norm_pull_one(grad_normed)
    grad_input = (
        (grad_hidden + grad_token_norm)
        .astype(jnp.bfloat16)
        .reshape(seqs_here, local_len, width)
    )
    next(down)
    g_bias_down = jnp.sum(grad_out_f, axis=0)
    g_bias_dense = jnp.sum(grad_hidden, axis=0)
    bias_total = jnp.sum(grad_mixed, axis=0, dtype=jnp.float32).reshape(heads_here, 3, HD)
    pair_total = jnp.concatenate([bias_total[:, :1], bias_total[:, 2:]], axis=1)
    g_pair_bias = lax.dynamic_update_slice_in_dim(
        jnp.zeros((H, 2, HD), jnp.float32), pair_total, lax.axis_index("seq") * heads_here, 0
    ).reshape(2 * H * HD)
    packed = pack(
        [
            g_gain_two,
            g_shift_two,
            g_bias_up,
            g_bias_down,
            g_bias_dense,
            g_gain_one,
            g_shift_one,
            g_pair_bias,
        ]
    )
    vector_sums = sum_all(order(packed), order, every)
    next(vector_sums)
    next(dense)
    next(down)
    next(vector_sums)
    next(up)
    next(qkv)
    next(vector_sums)
    next(down)
    next(dense)
    result = hidden + jnp.dot(gelu_out, w_down, preferred_element_type=jnp.float32) + bias_down
    output = order(result.astype(jnp.bfloat16)).reshape(seqs_here, local_len, width)
    next(vector_sums)
    next(up)
    next(qkv)
    next(dense)
    next(vector_sums)
    next(up)
    next(qkv)
    next(dense)
    next(up)
    next(qkv)
    next(dense)
    g_w_down = finish(down).astype(jnp.float32)
    small_sums = finish(vector_sums).reshape(-1)
    next(up)
    g_w_mixed = finish(qkv)
    g_w_mixed = gather(g_w_mixed, "seq")
    next(dense)
    g_w_up = finish(up).astype(jnp.float32)
    g_w_dense = finish(dense).astype(jnp.float32)
    g_w_mixed = jnp.moveaxis(g_w_mixed, 0, 1).astype(jnp.float32)
    g_w_mixed = g_w_mixed.reshape(-1, seq_ranks * columns)

    def own(packed, start, size):
        here = size // fsdp_ranks
        return lax.dynamic_slice_in_dim(packed, start + fsdp_rank * here, here, 0)

    hidden_units = bias_up.shape[0]
    g_gain_two = own(small_sums, 0, width)
    g_shift_two = own(small_sums, width, width)
    g_bias_up = own(small_sums, 2 * width, hidden_units)
    g_bias_down = own(small_sums, 2 * width + hidden_units, width)
    g_bias_dense = own(small_sums, 3 * width + hidden_units, width)
    g_gain_one = own(small_sums, 4 * width + hidden_units, width)
    g_shift_one = own(small_sums, 5 * width + hidden_units, width)
    g_pair_bias = own(small_sums, 6 * width + hidden_units, 2 * H * HD)

    return (
        output,
        grad_input,
        g_gain_one,
        g_shift_one,
        g_w_mixed,
        g_pair_bias,
        g_w_dense,
        g_bias_dense,
        g_gain_two,
        g_shift_two,
        g_w_up,
        g_bias_up,
        g_w_down,
        g_bias_down,
    )


def solution(mesh):
    placed = (
        P(("dp", "fsdp"), "seq", None),
        P(("dp", "fsdp"), None),
        P("fsdp"),
        P("fsdp"),
        P("fsdp", None),
        P("fsdp"),
        P("fsdp", None),
        P("fsdp"),
        P("fsdp"),
        P("fsdp"),
        P("fsdp", None),
        P("fsdp"),
        P("fsdp", None),
        P("fsdp"),
        P(("dp", "fsdp"), "seq", None),
    )
    return jax.shard_map(
        per_device,
        mesh=mesh,
        in_specs=placed,
        out_specs=(
            P(("dp", "fsdp"), "seq", None),
            P(("dp", "fsdp"), "seq", None),
            P("fsdp"),
            P("fsdp"),
            P("fsdp", None),
            P("fsdp"),
            P("fsdp", None),
            P("fsdp"),
            P("fsdp"),
            P("fsdp"),
            P("fsdp", None),
            P("fsdp"),
            P("fsdp", None),
            P("fsdp"),
        ),
        check_vma=False,
    )
```
